512 devices in a mesh: curve: 128 (over y, z, core), rep: 4 (over x).
Axes of the slice: x: 4, y: 4, z: 16, core: 2. Of those that a mesh axis runs over, the one named last changes fastest.
Arguments:
- offsets: float32 [65536, 3, 256], P(('curve', 'rep')), may hold values from -1 to 1
- masses: float32 [65536, 256], P(('curve', 'rep')), may hold values from 0.1 to 2
- destination: int32 [65536, 1], P(('curve', 'rep')), may hold values from 0 to 127; in each aligned block of 128 rows (0 to 127, 128 to 255, ...) at most 2 rows name the same one
- leaf_ids: int32 [65536], P(('curve', 'rep')), may hold values from 0 to 1023
Outputs:
- owned_offsets: float32 [131072, 3, 256], P(('curve', 'rep'))
- owned_masses: float32 [131072, 256], P(('curve', 'rep'))
- leaf_moments: float32 [35, 524288], P(None, ('curve', 'rep'))
- top_tree: float32 [35, 9344], replicated
The draws below stay inside these ranges and needn't reach their ends.
Inputs may be any that keep to these rules, and one draw needn't show every extreme that they name: `destination`: among the blocks of one device at most 2 name the same curve index, and in every draw some curve index is named by exactly 2 blocks of some device.
All inputs are finite; a program needn't handle non-finite values.
Results may differ from the reference program's by a relative error of at most 0.0001.
Values sent between devices are 32-bit elements; how exact they have to be, the bound alone decides.
A program may use at most 64 MiB of HBM per device.

```python
import math
import jax
import jax.numpy as jnp
import numpy as np
from jax import lax

PER_BLOCK = 256
BLOCKS_DEV = 128
LEAVES_DEV = 1024
PEER_SLOTS = 2
ALL_BLOCKS = 65536
ALL_OWNED = 131072
ALL_LEAVES = 524288
TOP_LEVEL = 1024
ROOT_LEVEL = 128
N_CURVE = 128
N_REP = 4
DEVICES = 512


def place_ends(values, key, least, top_value):
    dims = values.shape
    spot = [jax.random.randint(jax.random.fold_in(key, axis), (), 0, dims[axis]) for axis in range(len(dims))]
    values = values.at[tuple(spot)].set(least)
    longest = dims.index(max(dims))
    spot[longest] = (spot[longest] + 1) % dims[longest]
    return values.at[tuple(spot)].set(top_value)


def steps_of(own_key, shape, split, smallest, largest):
    level, own = 1.0, jax.random.fold_in(own_key, 6)
    for position, shards_of in split:
        draws = jnp.exp(jax.random.uniform(jax.random.fold_in(own, position), (shards_of,), jnp.float32, smallest / len(split), largest / len(split)))
        level = level * jnp.repeat(draws, shape[position] // shards_of).reshape([-1 if axis == position else 1 for axis in range(len(shape))])
    return level


def shared_out(own_key, own, number, rows, number_of, top, limit, slope):
    order = jax.random.permutation(own_key, number_of)
    packed, ordinary = shares(number_of, rows * top, limit, slope, True), shares(number_of, rows * top, limit, slope, False)
    places = jnp.arange(number_of)

    def named(tallies, turn):
        used = int((tallies > 0).sum())
        fixed = max(1, used // 4)
        moved = fixed + (places - fixed + turn * (used - fixed)) % max(1, number_of - fixed)
        return jnp.zeros((number_of,), jnp.int32).at[order[jnp.where(places < fixed, places, moved)]].set(jnp.asarray(tallies, jnp.int32))

    tallies = jnp.where(number % 4 == 0, named(packed, number // 4), named(ordinary, number - number // 4 - 1))
    mixed = jax.random.permutation(jax.random.fold_in(own, 3), number_of)
    donor, sink = mixed[0:number_of // 2 * 2:2], mixed[1:number_of // 2 * 2:2]
    slack = jnp.minimum(tallies[donor] - 1, limit - tallies[sink]) // 2
    slack = jnp.where((donor == order[0]) | (sink == order[0]) | (tallies[sink] == 0), 0, jnp.maximum(slack, 0))
    moved = jax.random.randint(jax.random.fold_in(own, 4), (number_of // 2,), 0, 1 << 20) % (slack + 1)
    tallies = tallies.at[donor].add(-moved).at[sink].add(moved)
    labels = jnp.searchsorted(jnp.cumsum(tallies), jnp.arange(rows * top), side="right").astype(jnp.int32)
    table = labels.reshape(top, rows).T
    table = table[jax.random.permutation(jax.random.fold_in(own, 1), rows)]
    turn = jax.random.randint(jax.random.fold_in(own, 2), (rows, 1), 0, top)
    return jnp.take_along_axis(table, (jnp.arange(top)[None, :] + turn) % top, axis=1)


def shares(count, total, reach, lean, full):
    weights = [(1 << 20) // math.isqrt(rank ** lean) + 1 for rank in range(1, count + 1)]
    largest = reach if full else min(reach, max(-(-total // count), total * weights[0] // sum(weights)))
    least = 1 if total - largest >= count - 1 else 0
    counts, surplus = [largest] + [least] * (count - 1), total - largest - least * (count - 1)
    while surplus > 0:
        candidates = [i for i in range(1, count) if counts[i] < largest] or [i for i in range(1, count) if counts[i] < reach]
        whole, remaining = sum([weights[i] for i in candidates]), surplus
        for i in candidates:
            extra = min(reach - counts[i], max(1, remaining * weights[i] // whole), surplus)
            counts[i] = counts[i] + extra
            surplus = surplus - extra
    return np.array(counts)


def setup_inputs(seed: int = 0) -> dict:
    streams_of = jax.random.split(jax.random.key(seed), 5)
    offsets = jnp.clip(jax.random.uniform(streams_of[0], (ALL_BLOCKS, 3, PER_BLOCK), jnp.float32, -1.0, 1.0) * steps_of(streams_of[0], (ALL_BLOCKS, 3, PER_BLOCK), ((0, 512),), -0.4, 0.0), -1.0, 1.0)
    masses = jnp.clip(jnp.exp(math.log(2.0) - 2.9957323 * jax.random.uniform(streams_of[1], (ALL_BLOCKS, PER_BLOCK), jnp.float32) ** steps_of(streams_of[1], (ALL_BLOCKS, PER_BLOCK), ((0, 512),), -0.2, 0.2)), 0.1, 2.0)
    destination_keys = jax.random.split(jax.random.fold_in(streams_of[2], 1), ALL_BLOCKS // BLOCKS_DEV)
    destination_turns = jax.random.permutation(jax.random.fold_in(streams_of[2], 3), ALL_BLOCKS // BLOCKS_DEV)
    destination = jax.vmap(lambda own, number: shared_out(jax.random.fold_in(streams_of[2], 2), own, number, BLOCKS_DEV, N_CURVE, 1, PEER_SLOTS, 2))(destination_keys, destination_turns).reshape((ALL_BLOCKS, 1))
    leaf_ids = place_ends(jax.random.randint(streams_of[3], (ALL_BLOCKS,), 0, LEAVES_DEV), jax.random.fold_in(streams_of[3], 1), 0, LEAVES_DEV - 1).astype(jnp.int32)
    return {"offsets": offsets, "masses": masses, "destination": destination, "leaf_ids": leaf_ids}


def moment_terms():
    listed = []
    for degree in range(5):
        for a in range(degree, -1, -1):
            for c in range(degree - a, -1, -1):
                listed.append((a, c, degree - a - c))
    return listed


def yz_pairs():
    return [(c, e) for c in range(5) for e in range(5 - c)]


def term_selection():
    pairs = yz_pairs()
    return np.array([a * 15 + pairs.index((c, e)) for (a, c, e) in moment_terms()], dtype=np.int32)


def octant_table():
    listed = moment_terms()
    table = np.zeros((8, 35, 35), dtype=np.float32)
    for octant in range(8):
        signs = (2 * (octant % 2) - 1, 2 * ((octant // 2) % 2) - 1, 2 * (octant // 4) - 1)
        for row, upper in enumerate(listed):
            for column, lower in enumerate(listed):
                if all(lower[i] <= upper[i] for i in range(3)):
                    value = 0.125 * 2.0 ** (-sum(upper))
                    for i in range(3):
                        value = value * math.comb(upper[i], lower[i]) * signs[i] ** (upper[i] - lower[i])
                    table[octant, row, column] = value
    return table


def lift_level(children):
    count = children.shape[1]
    shift_table = jnp.asarray(octant_table()).astype(children.dtype)
    grouped = children.reshape(children.shape[0], count // 8, 8)
    return jnp.einsum("oab,bno->an", shift_table, grouped, precision=lax.Precision.HIGHEST)


def block_moments(places, weights):
    count = places.shape[0]
    points = places.shape[2]
    group_size = 64 if count % 64 == 0 else count
    selection = term_selection()

    def block_group(parcel):
        spots, loads = parcel
        xcoord = spots[:, 0, :]
        ycoord = spots[:, 1, :]
        zcoord = spots[:, 2, :]
        xpowers = [loads]
        ypowers = [jnp.ones_like(ycoord)]
        zpowers = [jnp.ones_like(zcoord)]
        for level in range(4):
            xpowers.append(xpowers[-1] * xcoord)
            ypowers.append(ypowers[-1] * ycoord)
            zpowers.append(zpowers[-1] * zcoord)
        xstack = jnp.stack(xpowers)
        yzstack = jnp.stack([ypowers[c] * zpowers[e] for (c, e) in yz_pairs()])
        products = jnp.einsum("agp,kgp->gak", xstack, yzstack, precision=lax.Precision.HIGHEST) * (1.0 / points)
        return jnp.take(products.reshape(products.shape[0], 75), selection, axis=1)

    spots = places.reshape(count // group_size, group_size, 3, points)
    loads = weights.reshape(count // group_size, group_size, points)
    result = lax.map(block_group, (spots, loads))
    return result.reshape(count, 35)


def reference(offsets, masses, destination, leaf_ids):
    target = destination[:, 0].astype(jnp.int32)
    source = jnp.arange(ALL_BLOCKS, dtype=jnp.int32) // BLOCKS_DEV
    source_curve = source // N_REP
    source_rep = source % N_REP
    onehot = (target.reshape(DEVICES, BLOCKS_DEV)[:, :, None] == jnp.arange(N_CURVE, dtype=jnp.int32)[None, None, :]).astype(jnp.int32)
    before = jnp.cumsum(onehot, axis=1) - onehot
    within = jnp.sum(before * onehot, axis=2).reshape(ALL_BLOCKS)
    owner_rank = target * N_REP + source_rep
    slot_index = ((owner_rank * N_CURVE + source_curve) * PEER_SLOTS + within).astype(jnp.int32)
    owned_offsets = jnp.zeros((ALL_OWNED, 3, PER_BLOCK), jnp.float32).at[slot_index].set(offsets)
    owned_masses = jnp.zeros((ALL_OWNED, PER_BLOCK), jnp.float32).at[slot_index].set(masses)
    moments = block_moments(offsets, masses)
    leaf_index = (owner_rank * LEAVES_DEV + leaf_ids).astype(jnp.int32)
    leaf_moments = jax.ops.segment_sum(moments, leaf_index, num_segments=ALL_LEAVES).T
    level_one = lift_level(leaf_moments)
    level_two = lift_level(level_one)
    level_three = lift_level(level_two)
    padded = jnp.pad(level_three, ((0, 0), (0, ROOT_LEVEL * 8 - TOP_LEVEL)))
    level_four = lift_level(padded)
    top_tree = jnp.concatenate([level_two, level_three, level_four], axis=1)
    return owned_offsets, owned_masses, leaf_moments, top_tree
```

```python
import functools
import math

import jax
import jax.numpy as jnp
import numpy as np
from jax import lax
from jax.experimental import pallas as pl
from jax.experimental.pallas import tpu as pltpu
from jax.sharding import PartitionSpec as P

MESH = pl.DeviceIdType.MESH
NY, NZ, NX = 4, 16, 4
PEERS = 128
LEAVES_DEV = 1024
TERMS = 35
ROWS = 40
TILE_ROWS = 6
FIRST = 16


def moment_terms():
    listed = []
    for degree in range(5):
        for a in range(degree, -1, -1):
            for c in range(degree - a, -1, -1):
                listed.append((a, c, degree - a - c))
    return listed


def octant_table():
    listed = moment_terms()
    table = np.zeros((8, ROWS, ROWS), dtype=np.float32)
    for octant in range(8):
        signs = (2 * (octant % 2) - 1, 2 * (octant // 2 % 2) - 1, 2 * (octant // 4) - 1)
        for row, upper in enumerate(listed):
            for column, lower in enumerate(listed):
                if all(lower[i] <= upper[i] for i in range(3)):
                    value = 0.125 * 2.0 ** (-sum(upper))
                    for i in range(3):
                        value = (
                            value
                            * math.comb(upper[i], lower[i])
                            * signs[i] ** (upper[i] - lower[i])
                        )
                    table[octant, row, column] = value
    return table.reshape(8 * ROWS, ROWS)


def fold_table():
    table = np.zeros((64, TERMS * 8), dtype=np.float32)
    for term in range(TERMS):
        table[term, term * 8 : term * 8 + 8] = 1.0 / 256.0
    return table


def split3(value):
    high = value.astype(jnp.bfloat16)
    rest = value - high.astype(jnp.float32)
    middle = rest.astype(jnp.bfloat16)
    low = (rest - middle.astype(jnp.float32)).astype(jnp.bfloat16)
    return high, middle, low


NN = (((1,), (0,)), ((), ()))
NT = (((1,), (1,)), ((), ()))


def dot(a, b, dims):
    return lax.dot_general(a, b, dims, preferred_element_type=jnp.float32)


def dot_right(exact, value, dims=NN):
    high, middle, low = split3(value)
    return dot(exact, high, dims) + (dot(exact, middle, dims) + dot(exact, low, dims))


def dot_left(value, exact, dims=NN):
    high, middle, low = split3(value)
    return dot(high, exact, dims) + (dot(middle, exact, dims) + dot(low, exact, dims))


def iota(shape, axis):
    return lax.broadcasted_iota(jnp.int32, shape, axis)


def ones_where(mask):
    return jnp.where(mask, 1.0, 0.0).astype(jnp.bfloat16)


def raise_by(table, value, octant):
    moved = dot_right(table, value)
    total = jnp.zeros_like(value)
    for g in range(8):
        total = total + jnp.where(octant == g, moved[g * ROWS : (g + 1) * ROWS], 0.0)
    return total


def particle_moments(planes, fold):
    x, y, z, m = [jnp.transpose(plane) for plane in planes]
    sums = [None] * TERMS
    listed = moment_terms()
    for part in range(32):
        rows = slice(part * 8, part * 8 + 8)
        coordinates = (x[rows], y[rows], z[rows])
        made = {}
        for index, term in enumerate(listed):
            if sum(term) == 0:
                made[term] = m[rows]
            else:
                axis = [i for i in range(3) if term[i] > 0][0]
                below = tuple(term[i] - (1 if i == axis else 0) for i in range(3))
                made[term] = made[below] * coordinates[axis]
            sums[index] = made[term] if part == 0 else sums[index] + made[term]
    return dot_right(fold, jnp.concatenate(sums, axis=0))


def turn_blocks(value):
    sub = iota((8, 128), 0)
    group = iota((8, 128), 1) // 16
    for bit in (1, 2, 4):
        up = pltpu.roll(pltpu.roll(value, bit, 0), 128 - 16 * bit, 1)
        down = up if bit == 4 else pltpu.roll(pltpu.roll(value, 8 - bit, 0), 16 * bit, 1)
        moved = jnp.where((sub & bit) != 0, up, down)
        value = jnp.where(((sub ^ group) & bit) == 0, value, moved)
    return value


def exchange(
    offsets_hbm,
    masses_hbm,
    target_hbm,
    leaves_hbm,
    table_hbm,
    fold_hbm,
    landed,
    leaf_hbm,
    tree_hbm,
    offsets,
    masses,
    target,
    leaves,
    table_ref,
    fold_ref,
    bulk_size,
    slip_size,
    load_sems,
    packed,
    slips,
    got_slips,
    leaf_moments,
    tree,
    tiles,
    z_size,
    ready,
    leaf_sem,
    tree_sem,
    slip_out,
    slip_in,
    bulk_out,
    bulk_in,
    z_out,
    z_in,
    gather_out,
    gather_in,
    core_out,
    core_in,
):
    me = lax.axis_index("curve")
    x = lax.axis_index("rep")
    y, z, c = me // 32, (me // 2) % NZ, me % 2
    rank8 = c * NX + x

    def place(py, pz, pc):
        return (py * NZ + pz) * 2 + pc

    loads = [
        pltpu.make_async_copy(source, kept, load_sems.at[index])
        for index, (source, kept) in enumerate(
            (
                (target_hbm, target),
                (leaves_hbm, leaves),
                (masses_hbm, masses),
                (offsets_hbm, offsets),
                (fold_hbm, fold_ref),
                (table_hbm, table_ref),
            )
        )
    ]
    for load in loads:
        load.start()

    barrier = pltpu.get_barrier_semaphore()
    near = [(dy, dc) for dy in range(NY) for dc in range(2) if dy or dc]
    for dz in range(1, NZ):
        pl.semaphore_signal(
            barrier,
            inc=1,
            device_id={"curve": place(y, (z + dz) % NZ, c)},
            device_id_type=MESH,
        )
    for dy, dc in near:
        pl.semaphore_signal(
            barrier,
            inc=1,
            device_id={"curve": place((y + dy) % NY, z, (c + dc) % 2)},
            device_id_type=MESH,
        )
    group = [(dx, dc) for dx in range(NX) for dc in range(2) if dx or dc]
    for dx, dc in group:
        if dx:
            pl.semaphore_signal(
                barrier,
                inc=1,
                device_id={"curve": place(y, z, (c + dc) % 2), "rep": (x + dx) % NX},
                device_id_type=MESH,
            )

    for load in loads:
        load.wait()

    table = table_ref[...].astype(jnp.bfloat16)
    aim = target[...]
    leaf = leaves[...]
    named = ones_where(iota((PEERS, 128), 0) == aim)
    earlier = ones_where(iota((128, 128), 0) < iota((128, 128), 1))
    before = dot(named, earlier, NN)
    within = jnp.sum(before * named.astype(jnp.float32), axis=0, keepdims=True)
    slot = 2 * aim + within.astype(jnp.int32)

    planes = [offsets[0], offsets[1], offsets[2], masses[...]]
    moments = particle_moments(planes, fold_ref[...].astype(jnp.bfloat16))
    moments = jnp.where(iota((64, 128), 0) == TERMS, leaf.astype(jnp.float32), moments)
    nothing = jnp.zeros_like(moments)
    halves = jnp.concatenate(
        [
            jnp.concatenate([moments, nothing], axis=1),
            jnp.concatenate([nothing, moments], axis=1),
        ],
        axis=0,
    )
    twice = 2 * iota((128, 128), 0)
    picks = jnp.concatenate([ones_where(slot == twice), ones_where(slot == twice + 1)], axis=1)
    slips[...] = dot_right(picks, halves, NT)

    pl.semaphore_wait(barrier, 28)
    for dy, dc in near:
        pl.semaphore_signal(
            ready,
            inc=1,
            device_id={"curve": place((y + dy) % NY, z, (c + dc) % 2)},
            device_id_type=MESH,
        )

    spread = ones_where(iota((256, 128), 0) == slot)
    for index, plane in enumerate(planes):
        packed[index] = dot_right(spread, plane)

    pl.semaphore_wait(ready, 7)

    def peer(step):
        turn, inner = step // 8, 7 - step % 8
        dz = NZ // 2 + (1 - turn % 2) * (turn // 2) - (turn % 2) * ((turn + 1) // 2)
        return place((y + inner // 2) % NY, (z + dz) % NZ, (c + inner % 2) % 2)

    def send_slip(step, carry):
        to = peer(step)
        pltpu.make_async_remote_copy(
            slips.at[pl.ds(to, 1)],
            got_slips.at[pl.ds(me, 1)],
            slip_out,
            slip_in,
            device_id={"curve": to},
            device_id_type=MESH,
        ).start()
        return carry

    lax.fori_loop(0, PEERS - 1, send_slip, 0)
    pltpu.make_async_copy(
        slips.at[pl.ds(me, 1)], got_slips.at[pl.ds(me, 1)], slip_in
    ).start()

    def send_block(step, carry):
        to = peer(step)
        pltpu.make_async_remote_copy(
            packed.at[:, pl.ds(2 * to, 2)],
            landed.at[:, pl.ds(2 * me, 2)],
            bulk_out,
            bulk_in,
            device_id={"curve": to},
            device_id_type=MESH,
        ).start()
        return carry

    lax.fori_loop(0, FIRST, send_block, 0)
    pltpu.make_async_copy(
        packed.at[:, pl.ds(2 * me, 2)], landed.at[:, pl.ds(2 * me, 2)], bulk_in
    ).start()

    pltpu.make_async_copy(got_slips, got_slips, slip_in).wait()
    turned = jnp.transpose(got_slips[...])
    held = jnp.concatenate([turned[:ROWS], turned[64 : 64 + ROWS]], axis=1)
    cell = held[TERMS : TERMS + 1].astype(jnp.int32)
    one = raise_by(table, held, cell & 7)
    two = raise_by(table, one, (cell >> 3) & 7)
    three = raise_by(table, two, (cell >> 6) & 7)
    level_two = dot_left(two, ones_where(iota((128, 256), 0) % 16 == cell >> 6), NT)
    pair = dot_right(
        ones_where(iota((8, 256), 0) == cell >> 9),
        jnp.concatenate([three, jnp.zeros((64 - ROWS, 256), jnp.float32)], axis=0),
        NT,
    )
    own_lanes = iota((8, 128), 1) // 16 == iota((8, 128), 0)
    for row in range(5):
        tiles[y, z // 8, z % 8, row, pl.ds(rank8, 1)] = jnp.sum(
            jnp.where(own_lanes, level_two[8 * row : 8 * row + 8], 0.0),
            axis=0,
            keepdims=True,
        )
    tiles[y, z // 8, z % 8, 5, pl.ds(rank8, 1)] = jnp.concatenate([pair[0:1], pair[1:2]], axis=1)

    def to_z(dz, carry):
        mine = tiles.at[y, z // 8, z % 8, :, pl.ds(rank8, 1)]
        pltpu.make_async_remote_copy(
            mine,
            mine,
            z_out,
            z_in,
            device_id={"curve": place(y, (z + dz) % NZ, c)},
            device_id_type=MESH,
        ).start()
        return carry

    lax.fori_loop(1, NZ, to_z, 0)
    lax.fori_loop(FIRST, PEERS - 1, send_block, 0)

    leaf_moments[...] = dot_left(
        held, ones_where(iota((LEAVES_DEV, 256), 0) == cell), NT
    )[:TERMS]
    leaf_copy = pltpu.make_async_copy(leaf_moments, leaf_hbm, leaf_sem)
    leaf_copy.start()

    pltpu.make_async_copy(z_size, z_size, z_in).wait()

    def spread_tiles(along_y, along_x, turn):
        for step in range(1, NY):
            pltpu.make_async_remote_copy(
                along_y,
                along_y,
                gather_out.at[turn],
                gather_in.at[turn],
                device_id={"curve": place((y + step) % NY, z, c)},
                device_id_type=MESH,
            ).start()
            pltpu.make_async_remote_copy(
                along_x,
                along_x,
                gather_out.at[turn + 1],
                gather_in.at[turn + 1],
                device_id={"rep": (x + step) % NX},
                device_id_type=MESH,
            ).start()

    spread_tiles(
        tiles.at[y, 0, :, :, pl.ds(rank8, 1)],
        tiles.at[y, 1, :, :, pl.ds(rank8, 1)],
        0,
    )
    small = tiles.at[pl.ds(0, 3), 0, :, :, pl.ds(0, 1)]
    pltpu.make_async_copy(small, small, gather_in.at[0]).wait()
    pltpu.make_async_copy(small, small, gather_in.at[1]).wait()
    spread_tiles(
        tiles.at[y, 1, :, :, pl.ds(c * NX, NX)],
        tiles.at[:, 0, :, :, pl.ds(rank8, 1)],
        2,
    )
    large_y = tiles.at[pl.ds(0, 3), 1, :, :, pl.ds(0, 4)]
    large_x = tiles.at[pl.ds(0, 3), 0, :, :, pl.ds(0, 4)]
    pltpu.make_async_copy(large_y, large_y, gather_in.at[2]).wait()
    pltpu.make_async_copy(large_x, large_x, gather_in.at[3]).wait()
    half = tiles.at[:, :, :, :, pl.ds(c * NX, NX)]
    swap = pltpu.make_async_remote_copy(
        half,
        half,
        core_out,
        core_in,
        device_id={"curve": place(y, z, 1 - c)},
        device_id_type=MESH,
    )
    swap.start()
    swap.wait_recv()

    def write_column(index, carry):
        at = pl.ds(pl.multiple_of(index * 128, 128), 128)
        for row in range(5):
            whole = turn_blocks(tiles[index // 16, (index // 8) % 2, index % 8, row])
            if row < 4:
                tree[8 * row : 8 * row + 8, at] = whole
            else:
                tree[32:35, at] = whole[:3]
        return carry

    lax.fori_loop(0, NY * NZ, write_column, 0)
    pairs = jnp.transpose(tiles[:, :, :, 5].reshape(512, 128))
    stacked = jnp.concatenate(
        [
            jnp.concatenate(
                [pairs[:ROWS, 64 * j : 64 * j + 64], pairs[64 : 64 + ROWS, 64 * j : 64 * j + 64]],
                axis=1,
            )
            for j in range(8)
        ],
        axis=0,
    )
    wide = iota((128, 128), 0)
    thin = iota((128, 128), 1)
    folded = dot_left(stacked, ones_where(2 * (wide % 64) + wide // 64 == thin))
    whole_three = jnp.concatenate([folded[j * ROWS : (j + 1) * ROWS] for j in range(8)], axis=1)
    tree[:, 8192:9216] = whole_three[:TERMS]
    four = raise_by(table, whole_three, iota((1, 1024), 1) % 8)
    eight = iota((1024, 128), 0) // 8 == iota((1024, 128), 1)
    tree[:, 9216:9344] = dot_left(four, ones_where(eight))[:TERMS]
    tree_copy = pltpu.make_async_copy(tree, tree_hbm, tree_sem)
    tree_copy.start()

    pltpu.make_async_copy(landed, landed, bulk_in).wait()
    pltpu.make_async_copy(bulk_size, bulk_size, bulk_out).wait()
    pltpu.make_async_copy(slip_size, slip_size, slip_out).wait()
    pltpu.make_async_copy(z_size, z_size, z_out).wait()
    pltpu.make_async_copy(small, small, gather_out.at[0]).wait()
    pltpu.make_async_copy(small, small, gather_out.at[1]).wait()
    pltpu.make_async_copy(large_y, large_y, gather_out.at[2]).wait()
    pltpu.make_async_copy(large_x, large_x, gather_out.at[3]).wait()
    swap.wait_send()
    leaf_copy.wait()
    tree_copy.wait()


def store(
    landed,
    leaf_moments,
    tree,
    places,
    weights,
    leaf_out,
    tree_out,
    landed_kept,
    leaf_kept,
    tree_kept,
    in_sems,
    out_sems,
):
    steps = [(landed.at[p], landed_kept.at[p], places.at[p]) for p in range(3)]
    steps.append((landed.at[3], landed_kept.at[3], weights))
    for part in range(5):
        rows = pl.ds(8 * part, 8 if part < 4 else 3)
        steps.append((tree.at[rows], tree_kept.at[rows], tree_out.at[rows]))
    steps.append((leaf_moments, leaf_kept, leaf_out))
    ins = [
        pltpu.make_async_copy(source, kept, in_sems.at[index])
        for index, (source, kept, _) in enumerate(steps)
    ]
    outs = [
        pltpu.make_async_copy(kept, target, out_sems.at[index])
        for index, (_, kept, target) in enumerate(steps)
    ]
    for copy in ins:
        copy.start()
    for first, second in zip(ins, outs):
        first.wait()
        second.start()
    for copy in outs:
        copy.wait()


def shards(offsets, masses, destination, leaf_ids):
    landed, leaf_moments, tree = pl.pallas_call(
        exchange,
        out_shape=(
            jax.ShapeDtypeStruct((4, 256, 256), jnp.float32),
            jax.ShapeDtypeStruct((TERMS, LEAVES_DEV), jnp.float32),
            jax.ShapeDtypeStruct((TERMS, 9344), jnp.float32),
        ),
        in_specs=[pl.BlockSpec(memory_space=pltpu.HBM)] * 6,
        out_specs=(pl.BlockSpec(memory_space=pl.ANY),) * 3,
        scratch_shapes=[
            pltpu.VMEM((3, 128, 256), jnp.float32),
            pltpu.VMEM((128, 256), jnp.float32),
            pltpu.VMEM((1, 128), jnp.int32),
            pltpu.VMEM((1, 128), jnp.int32),
            pltpu.VMEM((8 * ROWS, ROWS), jnp.float32),
            pltpu.VMEM((64, TERMS * 8), jnp.float32),
            pltpu.VMEM((PEERS - 1, 8, 256), jnp.float32),
            pltpu.VMEM((PEERS - 1, 1, 128), jnp.float32),
            pltpu.SemaphoreType.DMA((6,)),
            pltpu.VMEM((4, 256, 256), jnp.float32),
            pltpu.VMEM((PEERS, 128), jnp.float32),
            pltpu.VMEM((PEERS, 128), jnp.float32),
            pltpu.VMEM((TERMS, LEAVES_DEV), jnp.float32),
            pltpu.VMEM((TERMS, 9344), jnp.float32),
            pltpu.VMEM((NY, 2, 8, TILE_ROWS, 8, 128), jnp.float32),
            pltpu.VMEM(((NZ - 1) * TILE_ROWS, 1, 128), jnp.float32),
            pltpu.SemaphoreType.REGULAR,
        ]
        + [pltpu.SemaphoreType.DMA] * 8
        + [pltpu.SemaphoreType.DMA((4,))] * 2
        + [pltpu.SemaphoreType.DMA] * 2,
        compiler_params=pltpu.CompilerParams(
            collective_id=1, has_side_effects=True, vmem_limit_bytes=60 * 1024 * 1024
        ),
        name="exchange",
    )(
        jnp.transpose(offsets, (1, 0, 2)),
        masses,
        destination.reshape(1, 128),
        leaf_ids.reshape(1, 128),
        jnp.asarray(octant_table()),
        jnp.asarray(fold_table()),
    )
    places, weights, leaf_moments, tree = pl.pallas_call(
        store,
        out_shape=(
            jax.ShapeDtypeStruct((3, 256, 256), jnp.float32),
            jax.ShapeDtypeStruct((256, 256), jnp.float32),
            jax.ShapeDtypeStruct((TERMS, LEAVES_DEV), jnp.float32),
            jax.ShapeDtypeStruct((TERMS, 9344), jnp.float32),
        ),
        in_specs=[pl.BlockSpec(memory_space=pl.ANY)] * 3,
        out_specs=(pl.BlockSpec(memory_space=pl.ANY),) * 4,
        scratch_shapes=[
            pltpu.VMEM((4, 256, 256), jnp.float32),
            pltpu.VMEM((TERMS, LEAVES_DEV), jnp.float32),
            pltpu.VMEM((TERMS, 9344), jnp.float32),
            pltpu.SemaphoreType.DMA((10,)),
            pltpu.SemaphoreType.DMA((10,)),
        ],
        compiler_params=pltpu.CompilerParams(vmem_limit_bytes=60 * 1024 * 1024),
        name="store",
    )(landed, leaf_moments, tree)
    return jnp.transpose(places, (1, 0, 2)), weights, leaf_moments, tree


def solution(mesh):
    placed = (
        P(("curve", "rep"), None, None),
        P(("curve", "rep"), None),
        P(("curve", "rep"), None),
        P(("curve", "rep")),
    )
    return jax.shard_map(
        shards,
        mesh=mesh,
        in_specs=placed,
        out_specs=(
            P(("curve", "rep"), None, None),
            P(("curve", "rep"), None),
            P(None, ("curve", "rep")),
            P(),
        ),
        check_vma=False,
    )
```

```python
import functools
import math

import jax
import jax.numpy as jnp
import numpy as np
from jax import lax
from jax.experimental import pallas as pl
from jax.experimental.pallas import tpu as pltpu
from jax.sharding import PartitionSpec as P

MESH = pl.DeviceIdType.MESH
NY, NZ, NX = 4, 16, 4
PEERS = 128
LEAVES_DEV = 1024
TERMS = 35
ROWS = 40
TILE_ROWS = 7


def moment_terms():
    listed = []
    for degree in range(5):
        for a in range(degree, -1, -1):
            for c in range(degree - a, -1, -1):
                listed.append((a, c, degree - a - c))
    return listed


def fold_table():
    table = np.zeros((64, TERMS * 8), dtype=np.float32)
    for term in range(TERMS):
        table[term, term * 8 : term * 8 + 8] = 1.0 / 256.0
    return table


def split3(value):
    high = value.astype(jnp.bfloat16)
    rest = value - high.astype(jnp.float32)
    middle = rest.astype(jnp.bfloat16)
    low = (rest - middle.astype(jnp.float32)).astype(jnp.bfloat16)
    return high, middle, low


NN = (((1,), (0,)), ((), ()))
NT = (((1,), (1,)), ((), ()))


def dot(a, b, dims):
    return lax.dot_general(a, b, dims, preferred_element_type=jnp.float32)


def dot_right(exact, value, dims=NN):
    high, middle, low = split3(value)
    return dot(exact, high, dims) + (dot(exact, middle, dims) + dot(exact, low, dims))


def dot_left(value, exact, dims=NN):
    high, middle, low = split3(value)
    return dot(high, exact, dims) + (dot(middle, exact, dims) + dot(low, exact, dims))


def iota(shape, axis):
    return lax.broadcasted_iota(jnp.int32, shape, axis)


def ones_where(mask):
    return jnp.where(mask, 1.0, 0.0).astype(jnp.bfloat16)


def signs(cell, levels):
    found = []
    for axis in range(3):
        total = None
        for level in range(levels):
            sign = 2 * ((cell >> (3 * level + axis)) & 1) - 1
            total = sign if level == 0 else total + (sign << level)
        found.append(total.astype(jnp.float32))
    return found


def lifted(rows, offsets, levels):
    listed = moment_terms()
    held = dict(zip(listed, rows))
    for axis in range(3):
        powers = [None, offsets[axis]]
        for _ in range(3):
            powers.append(powers[-1] * offsets[axis])
        factors = {}
        made = {}
        for term in listed:
            total = held[term]
            for step in range(1, term[axis] + 1):
                kind = (term[axis], step)
                if kind not in factors:
                    factors[kind] = powers[step] * float(math.comb(term[axis], step))
                lower = tuple(n - (step if i == axis else 0) for i, n in enumerate(term))
                total = total + factors[kind] * held[lower]
            made[term] = total
        held = made
    return [held[term] * (0.125**levels * 0.5 ** (levels * sum(term))) for term in listed]


def particle_moments(planes, fold):
    x, y, z, m = [jnp.transpose(plane) for plane in planes]
    sums = [None] * TERMS
    listed = moment_terms()
    for part in range(32):
        rows = slice(part * 8, part * 8 + 8)
        coordinates = (x[rows], y[rows], z[rows])
        made = {}
        for index, term in enumerate(listed):
            if sum(term) == 0:
                made[term] = m[rows]
            else:
                axis = [i for i in range(3) if term[i] > 0][0]
                below = tuple(term[i] - (1 if i == axis else 0) for i in range(3))
                made[term] = made[below] * coordinates[axis]
            sums[index] = made[term] if part == 0 else sums[index] + made[term]
    return dot_right(fold, jnp.concatenate(sums, axis=0))


def turn_blocks(value):
    sub = iota((8, 128), 0)
    group = iota((8, 128), 1) // 16
    for bit in (1, 2, 4):
        up = pltpu.roll(pltpu.roll(value, bit, 0), 128 - 16 * bit, 1)
        down = up if bit == 4 else pltpu.roll(pltpu.roll(value, 8 - bit, 0), 16 * bit, 1)
        moved = jnp.where((sub & bit) != 0, up, down)
        value = jnp.where(((sub ^ group) & bit) == 0, value, moved)
    return value


def exchange(
    offsets_hbm,
    masses_hbm,
    target_hbm,
    leaves_hbm,
    fold_hbm,
    landed,
    leaf_moments,
    tree,
    offsets,
    masses,
    target,
    leaves,
    fold_ref,
    bulk_size,
    slip_size,
    load_sems,
    packed,
    slips,
    got_slips,
    turned,
    raised,
    tiles,
    z_size,
    ready,
    slip_out,
    slip_in,
    bulk_out,
    bulk_in,
    z_out,
    z_in,
    gather_out,
    gather_in,
    core_out,
    core_in,
):
    me = lax.axis_index("curve")
    x = lax.axis_index("rep")
    y, z, c = me // 32, (me // 2) % NZ, me % 2
    rank8 = c * NX + x

    def place(py, pz, pc):
        return (py * NZ + pz) * 2 + pc

    loads = [
        pltpu.make_async_copy(source, kept, load_sems.at[index])
        for index, (source, kept) in enumerate(
            (
                (target_hbm, target),
                (leaves_hbm, leaves),
                (masses_hbm, masses),
                (offsets_hbm, offsets),
                (fold_hbm, fold_ref),
            )
        )
    ]
    for load in loads:
        load.start()

    barrier = pltpu.get_barrier_semaphore()
    near = [(dy, dc) for dy in range(NY) for dc in range(2) if dy or dc]
    for dz in range(1, NZ):
        pl.semaphore_signal(
            barrier,
            inc=1,
            device_id={"curve": place(y, (z + dz) % NZ, c)},
            device_id_type=MESH,
        )
    for dy, dc in near:
        pl.semaphore_signal(
            barrier,
            inc=1,
            device_id={"curve": place((y + dy) % NY, z, (c + dc) % 2)},
            device_id_type=MESH,
        )
    group = [(dx, dc) for dx in range(NX) for dc in range(2) if dx or dc]
    for dx, dc in group:
        if dx:
            pl.semaphore_signal(
                barrier,
                inc=1,
                device_id={"curve": place(y, z, (c + dc) % 2), "rep": (x + dx) % NX},
                device_id_type=MESH,
            )

    for load in loads:
        load.wait()

    aim = target[...]
    leaf = leaves[...]
    named = ones_where(iota((PEERS, 128), 0) == aim)
    earlier = ones_where(iota((128, 128), 0) < iota((128, 128), 1))
    before = dot(named, earlier, NN)
    within = jnp.sum(before * named.astype(jnp.float32), axis=0, keepdims=True)
    slot = 2 * aim + within.astype(jnp.int32)

    planes = [offsets[0], offsets[1], offsets[2], masses[...]]
    moments = particle_moments(planes, fold_ref[...].astype(jnp.bfloat16))
    moments = jnp.where(iota((64, 128), 0) == TERMS, leaf.astype(jnp.float32), moments)
    nothing = jnp.zeros_like(moments)
    halves = jnp.concatenate(
        [
            jnp.concatenate([moments, nothing], axis=1),
            jnp.concatenate([nothing, moments], axis=1),
        ],
        axis=0,
    )
    twice = 2 * iota((128, 128), 0)
    picks = jnp.concatenate([ones_where(slot == twice), ones_where(slot == twice + 1)], axis=1)
    slips[...] = dot_right(picks, halves, NT)

    pl.semaphore_wait(barrier, 28)
    for dy, dc in near:
        pl.semaphore_signal(
            ready,
            inc=1,
            device_id={"curve": place((y + dy) % NY, z, (c + dc) % 2)},
            device_id_type=MESH,
        )

    spread = ones_where(iota((256, 128), 0) == slot)
    for index, plane in enumerate(planes):
        packed[index] = dot_right(spread, plane)

    def peer(step, inner):
        dz = NZ // 2 + (1 - step % 2) * (step // 2) - (step % 2) * ((step + 1) // 2)
        return place((y + inner // 2) % NY, (z + dz) % NZ, (c + inner % 2) % 2)

    def send_slip(to):
        pltpu.make_async_remote_copy(
            slips.at[pl.ds(to, 1)],
            got_slips.at[pl.ds(me, 1)],
            slip_out,
            slip_in,
            device_id={"curve": to},
            device_id_type=MESH,
        ).start()

    def send_block(to):
        pltpu.make_async_remote_copy(
            packed.at[:, pl.ds(2 * to, 2)],
            landed.at[:, pl.ds(2 * me, 2)],
            bulk_out,
            bulk_in,
            device_id={"curve": to},
            device_id_type=MESH,
        ).start()

    def along_z(send):
        def body(step, carry):
            send(peer(step, 0))
            return carry

        lax.fori_loop(0, NZ - 1, body, 0)

    def all_others(send):
        def body(step, carry):
            send(peer(step // 7, 7 - step % 7))
            return carry

        lax.fori_loop(0, 7 * NZ, body, 0)

    along_z(send_slip)
    pl.semaphore_wait(ready, 7)
    all_others(send_slip)
    along_z(send_block)
    pltpu.make_async_copy(
        slips.at[pl.ds(me, 1)], got_slips.at[pl.ds(me, 1)], slip_in
    ).start()

    pltpu.make_async_copy(
        packed.at[:, pl.ds(2 * me, 2)], landed.at[:, pl.ds(2 * me, 2)], bulk_in
    ).start()

    pltpu.make_async_copy(got_slips, got_slips, slip_in).wait()
    turned[...] = jnp.transpose(got_slips[...])
    cell = jnp.concatenate(
        [turned[TERMS : TERMS + 1], turned[64 + TERMS : 65 + TERMS]], axis=1
    ).astype(jnp.int32)
    rows = [
        jnp.concatenate([turned[r : r + 1], turned[64 + r : 65 + r]], axis=1)
        for r in range(TERMS)
    ]
    raised[...] = jnp.zeros_like(raised)
    whole_cell = cell + 1024 * x
    for first, levels in ((0, 2), (64, 3), (128, 4)):
        for r, row in enumerate(lifted(rows, signs(whole_cell, levels), levels)):
            raised[first + r : first + r + 1] = row
    level_two = dot_left(
        raised[0:ROWS], ones_where(iota((128, 256), 0) % 16 == cell >> 6), NT
    )
    kind = iota((8, 256), 0)
    upper = dot_right(ones_where((kind == cell >> 9) | (kind == 2)), raised[64:192], NT)
    own_lanes = iota((8, 128), 1) // 16 == iota((8, 128), 0)
    for row in range(5):
        tiles[y, z // 8, z % 8, row, pl.ds(rank8, 1)] = jnp.sum(
            jnp.where(own_lanes, level_two[8 * row : 8 * row + 8], 0.0),
            axis=0,
            keepdims=True,
        )
    tiles[y, z // 8, z % 8, 5, pl.ds(rank8, 1)] = jnp.concatenate(
        [upper[0:1, :64], upper[1:2, :64]], axis=1
    )
    tiles[y, z // 8, z % 8, 6, pl.ds(rank8, 1)] = upper[2:3]

    def to_z(dz, carry):
        mine = tiles.at[y, z // 8, z % 8, :, pl.ds(rank8, 1)]
        pltpu.make_async_remote_copy(
            mine,
            mine,
            z_out,
            z_in,
            device_id={"curve": place(y, (z + dz) % NZ, c)},
            device_id_type=MESH,
        ).start()
        return carry

    lax.fori_loop(1, NZ, to_z, 0)
    all_others(send_block)

    held = jnp.concatenate([turned[:ROWS], turned[64 : 64 + ROWS]], axis=1)
    leaf_moments[...] = dot_left(
        held, ones_where(iota((LEAVES_DEV, 256), 0) == cell), NT
    )[:TERMS]

    pltpu.make_async_copy(z_size, z_size, z_in).wait()

    def spread_tiles(along_y, along_x, turn):
        for step in range(1, NY):
            pltpu.make_async_remote_copy(
                along_y,
                along_y,
                gather_out.at[turn],
                gather_in.at[turn],
                device_id={"curve": place((y + step) % NY, z, c)},
                device_id_type=MESH,
            ).start()
            pltpu.make_async_remote_copy(
                along_x,
                along_x,
                gather_out.at[turn + 1],
                gather_in.at[turn + 1],
                device_id={"rep": (x + step) % NX},
                device_id_type=MESH,
            ).start()

    spread_tiles(
        tiles.at[y, 0, :, :, pl.ds(rank8, 1)],
        tiles.at[y, 1, :, :, pl.ds(rank8, 1)],
        0,
    )
    small = tiles.at[pl.ds(0, 3), 0, :, :, pl.ds(0, 1)]
    pltpu.make_async_copy(small, small, gather_in.at[0]).wait()
    pltpu.make_async_copy(small, small, gather_in.at[1]).wait()
    spread_tiles(
        tiles.at[y, 1, :, :, pl.ds(c * NX, NX)],
        tiles.at[:, 0, :, :, pl.ds(rank8, 1)],
        2,
    )
    large_y = tiles.at[pl.ds(0, 3), 1, :, :, pl.ds(0, 4)]
    large_x = tiles.at[pl.ds(0, 3), 0, :, :, pl.ds(0, 4)]
    pltpu.make_async_copy(large_x, large_x, gather_in.at[3]).wait()
    swaps = []
    for half in range(2):
        if half:
            pltpu.make_async_copy(large_y, large_y, gather_in.at[2]).wait()
        mine = tiles.at[:, half, :, :, pl.ds(c * NX, NX)]
        swap = pltpu.make_async_remote_copy(
            mine,
            mine,
            core_out.at[half],
            core_in.at[half],
            device_id={"curve": place(y, z, 1 - c)},
            device_id_type=MESH,
        )
        swap.start()
        swaps.append(swap)

    for half in range(2):
        swaps[half].wait_recv()

        def write_column(index, carry, half=half):
            at_y, at_z = index // 8, index % 8
            column = at_y * NZ + half * 8 + at_z
            at = pl.ds(pl.multiple_of(column * 128, 128), 128)
            for row in range(5):
                whole = turn_blocks(tiles[at_y, half, at_z, row])
                if row < 4:
                    tree[8 * row : 8 * row + 8, at] = whole
                else:
                    tree[32:35, at] = whole[:3]
            return carry

        lax.fori_loop(0, NY * 8, write_column, 0)
    pairs = jnp.transpose(tiles[:, :, :, 5].reshape(512, 128))
    stacked = jnp.concatenate(
        [
            jnp.concatenate(
                [pairs[:ROWS, 64 * j : 64 * j + 64], pairs[64 : 64 + ROWS, 64 * j : 64 * j + 64]],
                axis=1,
            )
            for j in range(8)
        ],
        axis=0,
    )
    wide = iota((128, 128), 0)
    thin = iota((128, 128), 1)
    folded = dot_left(stacked, ones_where(2 * (wide % 64) + wide // 64 == thin))
    whole_three = jnp.concatenate([folded[j * ROWS : (j + 1) * ROWS] for j in range(8)], axis=1)
    tree[:, 8192:9216] = whole_three[:TERMS]
    tops = jnp.transpose(tiles[:, :, :, 6].reshape(512, 128))[64 : 64 + ROWS]
    four = iota((512, 128), 0) // 4 == iota((512, 128), 1)
    tree[:, 9216:9344] = dot_left(tops, ones_where(four))[:TERMS]
    pltpu.make_async_copy(landed, landed, bulk_in).wait()
    pltpu.make_async_copy(bulk_size, bulk_size, bulk_out).wait()
    pltpu.make_async_copy(slip_size, slip_size, slip_out).wait()
    pltpu.make_async_copy(z_size, z_size, z_out).wait()
    pltpu.make_async_copy(small, small, gather_out.at[0]).wait()
    pltpu.make_async_copy(small, small, gather_out.at[1]).wait()
    pltpu.make_async_copy(large_y, large_y, gather_out.at[2]).wait()
    pltpu.make_async_copy(large_x, large_x, gather_out.at[3]).wait()
    for swap in swaps:
        swap.wait_send()


def store(landed, leaf_moments, tree, places, weights, leaf_out, tree_out, sems):
    steps = [(landed.at[p], places.at[p]) for p in range(3)]
    steps.append((landed.at[3], weights))
    for part in range(5):
        rows = pl.ds(8 * part, 8 if part < 4 else 3)
        steps.append((tree.at[rows], tree_out.at[rows]))
    steps.append((leaf_moments, leaf_out))
    copies = [
        pltpu.make_async_copy(kept, target, sems.at[index])
        for index, (kept, target) in enumerate(steps)
    ]
    for copy in copies:
        copy.start()
    for copy in copies:
        copy.wait()


def shards(offsets, masses, destination, leaf_ids):
    vmem = pl.BlockSpec(memory_space=pltpu.VMEM)
    operands = (
        jnp.transpose(offsets, (1, 0, 2)),
        masses,
        destination.reshape(1, 128),
        leaf_ids.reshape(1, 128),
        jnp.asarray(fold_table()),
    )
    landed, leaf_moments, tree = pl.pallas_call(
        exchange,
        out_shape=(
            jax.ShapeDtypeStruct((4, 256, 256), jnp.float32),
            jax.ShapeDtypeStruct((TERMS, LEAVES_DEV), jnp.float32),
            jax.ShapeDtypeStruct((TERMS, 9344), jnp.float32),
        ),
        in_specs=[pl.BlockSpec(memory_space=pltpu.HBM)] * 5,
        out_specs=(vmem,) * 3,
        scratch_shapes=[
            pltpu.VMEM((3, 128, 256), jnp.float32),
            pltpu.VMEM((128, 256), jnp.float32),
            pltpu.VMEM((1, 128), jnp.int32),
            pltpu.VMEM((1, 128), jnp.int32),
            pltpu.VMEM((64, TERMS * 8), jnp.float32),
            pltpu.VMEM((PEERS - 1, 8, 256), jnp.float32),
            pltpu.VMEM((PEERS - 1, 1, 128), jnp.float32),
            pltpu.SemaphoreType.DMA((5,)),
            pltpu.VMEM((4, 256, 256), jnp.float32),
            pltpu.VMEM((PEERS, 128), jnp.float32),
            pltpu.VMEM((PEERS, 128), jnp.float32),
            pltpu.VMEM((PEERS, 128), jnp.float32),
            pltpu.VMEM((192, 256), jnp.float32),
            pltpu.VMEM((NY, 2, 8, TILE_ROWS, 8, 128), jnp.float32),
            pltpu.VMEM(((NZ - 1) * TILE_ROWS, 1, 128), jnp.float32),
            pltpu.SemaphoreType.REGULAR,
        ]
        + [pltpu.SemaphoreType.DMA] * 6
        + [pltpu.SemaphoreType.DMA((4,))] * 2
        + [pltpu.SemaphoreType.DMA((2,))] * 2,
        compiler_params=pltpu.CompilerParams(
            collective_id=1, has_side_effects=True, vmem_limit_bytes=40 * 1024 * 1024
        ),
        name="exchange",
    )(*[pltpu.with_memory_space_constraint(operand, pltpu.HBM) for operand in operands])
    places, weights, leaf_moments, tree = pl.pallas_call(
        store,
        out_shape=(
            jax.ShapeDtypeStruct((3, 256, 256), jnp.float32),
            jax.ShapeDtypeStruct((256, 256), jnp.float32),
            jax.ShapeDtypeStruct((TERMS, LEAVES_DEV), jnp.float32),
            jax.ShapeDtypeStruct((TERMS, 9344), jnp.float32),
        ),
        in_specs=[vmem] * 3,
        out_specs=(pl.BlockSpec(memory_space=pl.ANY),) * 4,
        scratch_shapes=[pltpu.SemaphoreType.DMA((10,))],
        compiler_params=pltpu.CompilerParams(vmem_limit_bytes=40 * 1024 * 1024),
        name="store",
    )(landed, leaf_moments, tree)
    return jnp.transpose(places, (1, 0, 2)), weights, leaf_moments, tree


def solution(mesh):
    placed = (
        P(("curve", "rep"), None, None),
        P(("curve", "rep"), None),
        P(("curve", "rep"), None),
        P(("curve", "rep")),
    )
    return jax.shard_map(
        shards,
        mesh=mesh,
        in_specs=placed,
        out_specs=(
            P(("curve", "rep"), None, None),
            P(("curve", "rep"), None),
            P(None, ("curve", "rep")),
            P(),
        ),
        check_vma=False,
    )
```

```python
import functools
import math

import jax
import jax.numpy as jnp
import numpy as np
from jax import lax
from jax.experimental import pallas as pl
from jax.experimental.pallas import tpu as pltpu
from jax.sharding import PartitionSpec as P

MESH = pl.DeviceIdType.MESH
NY, NZ, NX = 4, 16, 4
PEERS = 128
LEAVES_DEV = 1024
TERMS = 35
ROWS = 40
SPARE = 48
TILE_ROWS = 5


def moment_terms():
    listed = []
    for degree in range(5):
        for a in range(degree, -1, -1):
            for c in range(degree - a, -1, -1):
                listed.append((a, c, degree - a - c))
    return listed


def fold_table():
    table = np.zeros((64, TERMS * 8), dtype=np.float32)
    for term in range(TERMS):
        table[term, term * 8 : term * 8 + 8] = 1.0 / 256.0
    return table


def split3(value):
    high = value.astype(jnp.bfloat16)
    rest = value - high.astype(jnp.float32)
    middle = rest.astype(jnp.bfloat16)
    low = (rest - middle.astype(jnp.float32)).astype(jnp.bfloat16)
    return high, middle, low


NN = (((1,), (0,)), ((), ()))
NT = (((1,), (1,)), ((), ()))


def dot(a, b, dims):
    return lax.dot_general(a, b, dims, preferred_element_type=jnp.float32)


def dot_right(exact, value, dims=NN):
    high, middle, low = split3(value)
    return dot(exact, high, dims) + (dot(exact, middle, dims) + dot(exact, low, dims))


def dot_left(value, exact, dims=NN):
    high, middle, low = split3(value)
    return dot(high, exact, dims) + (dot(middle, exact, dims) + dot(low, exact, dims))


def iota(shape, axis):
    return lax.broadcasted_iota(jnp.int32, shape, axis)


def ones_where(mask):
    return jnp.where(mask, 1.0, 0.0).astype(jnp.bfloat16)


def signs(cell, levels):
    found = []
    for axis in range(3):
        total = None
        for level in range(levels):
            sign = 2 * ((cell >> (3 * level + axis)) & 1) - 1
            total = sign if level == 0 else total + (sign << level)
        found.append(total.astype(jnp.float32))
    return found


def lifted(rows, offsets, levels):
    listed = moment_terms()
    held = dict(zip(listed, rows))
    for axis in range(3):
        powers = [None, offsets[axis]]
        for _ in range(3):
            powers.append(powers[-1] * offsets[axis])
        factors = {}
        made = {}
        for term in listed:
            total = held[term]
            for step in range(1, term[axis] + 1):
                kind = (term[axis], step)
                if kind not in factors:
                    factors[kind] = powers[step] * float(math.comb(term[axis], step))
                lower = tuple(n - (step if i == axis else 0) for i, n in enumerate(term))
                total = total + factors[kind] * held[lower]
            made[term] = total
        held = made
    return [held[term] * (0.125**levels * 0.5 ** (levels * sum(term))) for term in listed]


def particle_moments(planes, fold):
    x, y, z, m = [jnp.transpose(plane) for plane in planes]
    sums = [None] * TERMS
    listed = moment_terms()
    for part in range(32):
        rows = slice(part * 8, part * 8 + 8)
        coordinates = (x[rows], y[rows], z[rows])
        made = {}
        for index, term in enumerate(listed):
            if sum(term) == 0:
                made[term] = m[rows]
            else:
                axis = [i for i in range(3) if term[i] > 0][0]
                below = tuple(term[i] - (1 if i == axis else 0) for i in range(3))
                made[term] = made[below] * coordinates[axis]
            sums[index] = made[term] if part == 0 else sums[index] + made[term]
    return dot_right(fold, jnp.concatenate(sums, axis=0))


def turn_blocks(value):
    sub = iota((8, 128), 0)
    group = iota((8, 128), 1) // 16
    for bit in (1, 2, 4):
        up = pltpu.roll(pltpu.roll(value, bit, 0), 128 - 16 * bit, 1)
        down = up if bit == 4 else pltpu.roll(pltpu.roll(value, 8 - bit, 0), 16 * bit, 1)
        moved = jnp.where((sub & bit) != 0, up, down)
        value = jnp.where(((sub ^ group) & bit) == 0, value, moved)
    return value


def exchange(
    offsets_hbm,
    masses_hbm,
    target_hbm,
    leaves_hbm,
    fold_hbm,
    landed,
    leaf_moments,
    tree,
    offsets,
    masses,
    target,
    leaves,
    fold_ref,
    bulk_size,
    slip_size,
    load_sems,
    packed,
    slips,
    got_slips,
    turned,
    raised,
    tiles,
    z_size,
    ready,
    slip_out,
    slip_in,
    bulk_out,
    bulk_in,
    z_out,
    z_in,
    gather_out,
    gather_in,
    core_out,
    core_in,
):
    me = lax.axis_index("curve")
    x = lax.axis_index("rep")
    y, z, c = me // 32, (me // 2) % NZ, me % 2
    rank8 = c * NX + x

    def place(py, pz, pc):
        return (py * NZ + pz) * 2 + pc

    loads = [
        pltpu.make_async_copy(source, kept, load_sems.at[index])
        for index, (source, kept) in enumerate(
            (
                (target_hbm, target),
                (leaves_hbm, leaves),
                (masses_hbm, masses),
                (offsets_hbm, offsets),
                (fold_hbm, fold_ref),
            )
        )
    ]
    for load in loads:
        load.start()

    barrier = pltpu.get_barrier_semaphore()
    near = [(dy, dc) for dy in range(NY) for dc in range(2) if dy or dc]
    for dz in range(1, NZ):
        pl.semaphore_signal(
            barrier,
            inc=1,
            device_id={"curve": place(y, (z + dz) % NZ, c)},
            device_id_type=MESH,
        )
    for dy, dc in near:
        pl.semaphore_signal(
            barrier,
            inc=1,
            device_id={"curve": place((y + dy) % NY, z, (c + dc) % 2)},
            device_id_type=MESH,
        )
    group = [(dx, dc) for dx in range(NX) for dc in range(2) if dx or dc]
    for dx, dc in group:
        if dx:
            pl.semaphore_signal(
                barrier,
                inc=1,
                device_id={"curve": place(y, z, (c + dc) % 2), "rep": (x + dx) % NX},
                device_id_type=MESH,
            )

    for load in loads:
        load.wait()

    aim = target[...]
    leaf = leaves[...]
    named = ones_where(iota((PEERS, 128), 0) == aim)
    earlier = ones_where(iota((128, 128), 0) < iota((128, 128), 1))
    before = dot(named, earlier, NN)
    within = jnp.sum(before * named.astype(jnp.float32), axis=0, keepdims=True)
    slot = 2 * aim + within.astype(jnp.int32)

    planes = [offsets[0], offsets[1], offsets[2], masses[...]]
    moments = particle_moments(planes, fold_ref[...].astype(jnp.bfloat16))
    moments = jnp.where(iota((64, 128), 0) == TERMS, leaf.astype(jnp.float32), moments)
    nothing = jnp.zeros_like(moments)
    halves = jnp.concatenate(
        [
            jnp.concatenate([moments, nothing], axis=1),
            jnp.concatenate([nothing, moments], axis=1),
        ],
        axis=0,
    )
    twice = 2 * iota((128, 128), 0)
    picks = jnp.concatenate([ones_where(slot == twice), ones_where(slot == twice + 1)], axis=1)
    slips[...] = dot_right(picks, halves, NT)

    pl.semaphore_wait(barrier, 28)
    for dy, dc in near:
        pl.semaphore_signal(
            ready,
            inc=1,
            device_id={"curve": place((y + dy) % NY, z, (c + dc) % 2)},
            device_id_type=MESH,
        )

    spread = ones_where(iota((256, 128), 0) == slot)
    for index, plane in enumerate(planes):
        packed[index] = dot_right(spread, plane)

    def peer(step, inner):
        dz = NZ // 2 + (1 - step % 2) * (step // 2) - (step % 2) * ((step + 1) // 2)
        return place((y + inner // 2) % NY, (z + dz) % NZ, (c + inner % 2) % 2)

    def send_slip(to):
        pltpu.make_async_remote_copy(
            slips.at[pl.ds(to, 1)],
            got_slips.at[pl.ds(me, 1)],
            slip_out,
            slip_in,
            device_id={"curve": to},
            device_id_type=MESH,
        ).start()

    def send_block(to):
        pltpu.make_async_remote_copy(
            packed.at[:, pl.ds(2 * to, 2)],
            landed.at[:, pl.ds(2 * me, 2)],
            bulk_out,
            bulk_in,
            device_id={"curve": to},
            device_id_type=MESH,
        ).start()

    def along_z(send):
        def body(step, carry):
            send(peer(step, 0))
            return carry

        lax.fori_loop(0, NZ - 1, body, 0)

    def all_others(send):
        def body(step, carry):
            send(peer(step // 7, 7 - step % 7))
            return carry

        lax.fori_loop(0, 7 * NZ, body, 0)

    along_z(send_slip)
    pl.semaphore_wait(ready, 7)
    all_others(send_slip)
    along_z(send_block)
    pltpu.make_async_copy(
        slips.at[pl.ds(me, 1)], got_slips.at[pl.ds(me, 1)], slip_in
    ).start()

    pltpu.make_async_copy(
        packed.at[:, pl.ds(2 * me, 2)], landed.at[:, pl.ds(2 * me, 2)], bulk_in
    ).start()

    pltpu.make_async_copy(got_slips, got_slips, slip_in).wait()
    turned[...] = jnp.transpose(got_slips[...])
    cell = jnp.concatenate(
        [turned[TERMS : TERMS + 1], turned[64 + TERMS : 65 + TERMS]], axis=1
    ).astype(jnp.int32)
    rows = [
        jnp.concatenate([turned[r : r + 1], turned[64 + r : 65 + r]], axis=1)
        for r in range(TERMS)
    ]
    raised[...] = jnp.zeros_like(raised)
    for r, row in enumerate(lifted(rows, signs(cell, 2), 2)):
        raised[r : r + 1] = row
    for r, row in enumerate(lifted(rows, signs(cell, 3), 3)):
        for first in (64 + SPARE, 64 + SPARE + TERMS):
            raised[first + r : first + r + 1] = row
    level_two = dot_left(
        raised[0:ROWS], ones_where(iota((128, 256), 0) % 16 == cell >> 6), NT
    )
    upper = dot_right(ones_where(iota((8, 256), 0) == cell >> 9), raised[64:192], NT)
    own_lanes = iota((8, 128), 1) // 16 == iota((8, 128), 0)
    flat = [
        jnp.sum(
            jnp.where(own_lanes, level_two[8 * row : 8 * row + 8], 0.0),
            axis=0,
            keepdims=True,
        )
        for row in range(TILE_ROWS)
    ]
    lane = iota((1, 128), 1)
    flat[4] = jnp.where(
        lane < SPARE, flat[4], jnp.where(lane < SPARE + TERMS, upper[0:1], upper[1:2])
    )
    for row in range(TILE_ROWS):
        tiles[y, z // 8, z % 8, row, pl.ds(rank8, 1)] = flat[row]

    def to_z(dz, carry):
        mine = tiles.at[y, z // 8, z % 8, :, pl.ds(rank8, 1)]
        pltpu.make_async_remote_copy(
            mine,
            mine,
            z_out,
            z_in,
            device_id={"curve": place(y, (z + dz) % NZ, c)},
            device_id_type=MESH,
        ).start()
        return carry

    lax.fori_loop(1, NZ, to_z, 0)
    all_others(send_block)

    held = jnp.concatenate([turned[:ROWS], turned[64 : 64 + ROWS]], axis=1)
    leaf_moments[...] = dot_left(
        held, ones_where(iota((LEAVES_DEV, 256), 0) == cell), NT
    )[:TERMS]

    pltpu.make_async_copy(z_size, z_size, z_in).wait()

    def spread_tiles(along_y, along_x, turn):
        for step in range(1, NY):
            pltpu.make_async_remote_copy(
                along_y,
                along_y,
                gather_out.at[turn],
                gather_in.at[turn],
                device_id={"curve": place((y + step) % NY, z, c)},
                device_id_type=MESH,
            ).start()
            pltpu.make_async_remote_copy(
                along_x,
                along_x,
                gather_out.at[turn + 1],
                gather_in.at[turn + 1],
                device_id={"rep": (x + step) % NX},
                device_id_type=MESH,
            ).start()

    spread_tiles(
        tiles.at[y, 0, :, :, pl.ds(rank8, 1)],
        tiles.at[y, 1, :, :, pl.ds(rank8, 1)],
        0,
    )
    small = tiles.at[pl.ds(0, 3), 0, :, :, pl.ds(0, 1)]
    pltpu.make_async_copy(small, small, gather_in.at[0]).wait()
    pltpu.make_async_copy(small, small, gather_in.at[1]).wait()
    spread_tiles(
        tiles.at[y, 1, :, :, pl.ds(c * NX, NX)],
        tiles.at[:, 0, :, :, pl.ds(rank8, 1)],
        2,
    )
    large_y = tiles.at[pl.ds(0, 3), 1, :, :, pl.ds(0, 4)]
    large_x = tiles.at[pl.ds(0, 3), 0, :, :, pl.ds(0, 4)]
    pltpu.make_async_copy(large_x, large_x, gather_in.at[3]).wait()
    swaps = []
    for half in range(2):
        if half:
            pltpu.make_async_copy(large_y, large_y, gather_in.at[2]).wait()
        mine = tiles.at[:, half, :, :, pl.ds(c * NX, NX)]
        swap = pltpu.make_async_remote_copy(
            mine,
            mine,
            core_out.at[half],
            core_in.at[half],
            device_id={"curve": place(y, z, 1 - c)},
            device_id_type=MESH,
        )
        swap.start()
        swaps.append(swap)

    for half in range(2):
        swaps[half].wait_recv()

        def write_column(index, carry, half=half):
            at_y, at_z = index // 8, index % 8
            column = at_y * NZ + half * 8 + at_z
            at = pl.ds(pl.multiple_of(column * 128, 128), 128)
            for row in range(5):
                whole = turn_blocks(tiles[at_y, half, at_z, row])
                if row < 4:
                    tree[8 * row : 8 * row + 8, at] = whole
                else:
                    tree[32:35, at] = whole[:3]
            return carry

        lax.fori_loop(0, NY * 8, write_column, 0)
    pairs = jnp.transpose(tiles[:, :, :, 4].reshape(512, 128))
    stacked = jnp.concatenate(
        [
            jnp.concatenate(
                [
                    pairs[SPARE : SPARE + ROWS, 64 * j : 64 * j + 64],
                    pairs[SPARE + TERMS : SPARE + TERMS + ROWS, 64 * j : 64 * j + 64],
                ],
                axis=1,
            )
            for j in range(8)
        ],
        axis=0,
    )
    wide = iota((128, 128), 0)
    thin = iota((128, 128), 1)
    folded = dot_left(stacked, ones_where(2 * (wide % 64) + wide // 64 == thin))
    whole_three = jnp.concatenate([folded[j * ROWS : (j + 1) * ROWS] for j in range(8)], axis=1)
    tree[:, 8192:9216] = whole_three[:TERMS]
    below = [tree[r : r + 1, 8192:9216] for r in range(TERMS)]
    four = jnp.concatenate(lifted(below, signs(iota((1, 1024), 1), 1), 1), axis=0)
    eight = iota((1024, 128), 0) // 8 == iota((1024, 128), 1)
    tree[:, 9216:9344] = dot_left(four, ones_where(eight))

    pltpu.make_async_copy(landed, landed, bulk_in).wait()
    pltpu.make_async_copy(bulk_size, bulk_size, bulk_out).wait()
    pltpu.make_async_copy(slip_size, slip_size, slip_out).wait()
    pltpu.make_async_copy(z_size, z_size, z_out).wait()
    pltpu.make_async_copy(small, small, gather_out.at[0]).wait()
    pltpu.make_async_copy(small, small, gather_out.at[1]).wait()
    pltpu.make_async_copy(large_y, large_y, gather_out.at[2]).wait()
    pltpu.make_async_copy(large_x, large_x, gather_out.at[3]).wait()
    for swap in swaps:
        swap.wait_send()


def store(landed, leaf_moments, tree, places, weights, leaf_out, tree_out, sems):
    steps = [(landed.at[p], places.at[p]) for p in range(3)]
    steps.append((landed.at[3], weights))
    for part in range(5):
        rows = pl.ds(8 * part, 8 if part < 4 else 3)
        steps.append((tree.at[rows], tree_out.at[rows]))
    steps.append((leaf_moments, leaf_out))
    copies = [
        pltpu.make_async_copy(kept, target, sems.at[index])
        for index, (kept, target) in enumerate(steps)
    ]
    for copy in copies:
        copy.start()
    for copy in copies:
        copy.wait()


def shards(offsets, masses, destination, leaf_ids):
    vmem = pl.BlockSpec(memory_space=pltpu.VMEM)
    operands = (
        jnp.transpose(offsets, (1, 0, 2)),
        masses,
        destination.reshape(1, 128),
        leaf_ids.reshape(1, 128),
        jnp.asarray(fold_table()),
    )
    landed, leaf_moments, tree = pl.pallas_call(
        exchange,
        out_shape=(
            jax.ShapeDtypeStruct((4, 256, 256), jnp.float32),
            jax.ShapeDtypeStruct((TERMS, LEAVES_DEV), jnp.float32),
            jax.ShapeDtypeStruct((TERMS, 9344), jnp.float32),
        ),
        in_specs=[pl.BlockSpec(memory_space=pltpu.HBM)] * 5,
        out_specs=(vmem,) * 3,
        scratch_shapes=[
            pltpu.VMEM((3, 128, 256), jnp.float32),
            pltpu.VMEM((128, 256), jnp.float32),
            pltpu.VMEM((1, 128), jnp.int32),
            pltpu.VMEM((1, 128), jnp.int32),
            pltpu.VMEM((64, TERMS * 8), jnp.float32),
            pltpu.VMEM((PEERS - 1, 8, 256), jnp.float32),
            pltpu.VMEM((PEERS - 1, 1, 128), jnp.float32),
            pltpu.SemaphoreType.DMA((5,)),
            pltpu.VMEM((4, 256, 256), jnp.float32),
            pltpu.VMEM((PEERS, 128), jnp.float32),
            pltpu.VMEM((PEERS, 128), jnp.float32),
            pltpu.VMEM((PEERS, 128), jnp.float32),
            pltpu.VMEM((192, 256), jnp.float32),
            pltpu.VMEM((NY, 2, 8, TILE_ROWS, 8, 128), jnp.float32),
            pltpu.VMEM(((NZ - 1) * TILE_ROWS, 1, 128), jnp.float32),
            pltpu.SemaphoreType.REGULAR,
        ]
        + [pltpu.SemaphoreType.DMA] * 6
        + [pltpu.SemaphoreType.DMA((4,))] * 2
        + [pltpu.SemaphoreType.DMA((2,))] * 2,
        compiler_params=pltpu.CompilerParams(
            collective_id=1, has_side_effects=True, vmem_limit_bytes=40 * 1024 * 1024
        ),
        name="exchange",
    )(*[pltpu.with_memory_space_constraint(operand, pltpu.HBM) for operand in operands])
    places, weights, leaf_moments, tree = pl.pallas_call(
        store,
        out_shape=(
            jax.ShapeDtypeStruct((3, 256, 256), jnp.float32),
            jax.ShapeDtypeStruct((256, 256), jnp.float32),
            jax.ShapeDtypeStruct((TERMS, LEAVES_DEV), jnp.float32),
            jax.ShapeDtypeStruct((TERMS, 9344), jnp.float32),
        ),
        in_specs=[vmem] * 3,
        out_specs=(pl.BlockSpec(memory_space=pl.ANY),) * 4,
        scratch_shapes=[pltpu.SemaphoreType.DMA((10,))],
        compiler_params=pltpu.CompilerParams(vmem_limit_bytes=40 * 1024 * 1024),
        name="store",
    )(landed, leaf_moments, tree)
    return jnp.transpose(places, (1, 0, 2)), weights, leaf_moments, tree


def solution(mesh):
    placed = (
        P(("curve", "rep"), None, None),
        P(("curve", "rep"), None),
        P(("curve", "rep"), None),
        P(("curve", "rep")),
    )
    return jax.shard_map(
        shards,
        mesh=mesh,
        in_specs=placed,
        out_specs=(
            P(("curve", "rep"), None, None),
            P(("curve", "rep"), None),
            P(None, ("curve", "rep")),
            P(),
        ),
        check_vma=False,
    )
```

```python
import functools
import math

import jax
import jax.numpy as jnp
import numpy as np
from jax import lax
from jax.experimental import pallas as pl
from jax.experimental.pallas import tpu as pltpu
from jax.sharding import PartitionSpec as P

MESH = pl.DeviceIdType.MESH
NY, NZ, NX = 4, 16, 4
PEERS = 128
LEAVES_DEV = 1024
TERMS = 35
ROWS = 40
SPARE = 48
TILE_ROWS = 5


def moment_terms():
    listed = []
    for degree in range(5):
        for a in range(degree, -1, -1):
            for c in range(degree - a, -1, -1):
                listed.append((a, c, degree - a - c))
    return listed


def fold_table():
    table = np.zeros((64, TERMS * 8), dtype=np.float32)
    for term in range(TERMS):
        table[term, term * 8 : term * 8 + 8] = 1.0 / 256.0
    return table


def split3(value):
    high = value.astype(jnp.bfloat16)
    rest = value - high.astype(jnp.float32)
    middle = rest.astype(jnp.bfloat16)
    low = (rest - middle.astype(jnp.float32)).astype(jnp.bfloat16)
    return high, middle, low


NN = (((1,), (0,)), ((), ()))
NT = (((1,), (1,)), ((), ()))


def dot(a, b, dims):
    return lax.dot_general(a, b, dims, preferred_element_type=jnp.float32)


def dot_right(exact, value, dims=NN):
    high, middle, low = split3(value)
    return dot(exact, high, dims) + (dot(exact, middle, dims) + dot(exact, low, dims))


def dot_left(value, exact, dims=NN):
    high, middle, low = split3(value)
    return dot(high, exact, dims) + (dot(middle, exact, dims) + dot(low, exact, dims))


def iota(shape, axis):
    return lax.broadcasted_iota(jnp.int32, shape, axis)


def ones_where(mask):
    return jnp.where(mask, 1.0, 0.0).astype(jnp.bfloat16)


def signs(cell, levels):
    found = []
    for axis in range(3):
        total = None
        for level in range(levels):
            sign = 2 * ((cell >> (3 * level + axis)) & 1) - 1
            total = sign if level == 0 else total + (sign << level)
        found.append(total.astype(jnp.float32))
    return found


def lifted(rows, offsets, levels):
    listed = moment_terms()
    held = dict(zip(listed, rows))
    for axis in range(3):
        powers = [None, offsets[axis]]
        for _ in range(3):
            powers.append(powers[-1] * offsets[axis])
        factors = {}
        made = {}
        for term in listed:
            total = held[term]
            for step in range(1, term[axis] + 1):
                kind = (term[axis], step)
                if kind not in factors:
                    factors[kind] = powers[step] * float(math.comb(term[axis], step))
                lower = tuple(n - (step if i == axis else 0) for i, n in enumerate(term))
                total = total + factors[kind] * held[lower]
            made[term] = total
        held = made
    return [held[term] * (0.125**levels * 0.5 ** (levels * sum(term))) for term in listed]


def particle_moments(planes, fold):
    x, y, z, m = [jnp.transpose(plane) for plane in planes]
    sums = [None] * TERMS
    listed = moment_terms()
    for part in range(32):
        rows = slice(part * 8, part * 8 + 8)
        coordinates = (x[rows], y[rows], z[rows])
        made = {}
        for index, term in enumerate(listed):
            if sum(term) == 0:
                made[term] = m[rows]
            else:
                axis = [i for i in range(3) if term[i] > 0][0]
                below = tuple(term[i] - (1 if i == axis else 0) for i in range(3))
                made[term] = made[below] * coordinates[axis]
            sums[index] = made[term] if part == 0 else sums[index] + made[term]
    return dot_right(fold, jnp.concatenate(sums, axis=0))


def turn_blocks(value):
    sub = iota((8, 128), 0)
    group = iota((8, 128), 1) // 16
    for bit in (1, 2, 4):
        up = pltpu.roll(pltpu.roll(value, bit, 0), 128 - 16 * bit, 1)
        down = up if bit == 4 else pltpu.roll(pltpu.roll(value, 8 - bit, 0), 16 * bit, 1)
        moved = jnp.where((sub & bit) != 0, up, down)
        value = jnp.where(((sub ^ group) & bit) == 0, value, moved)
    return value


def exchange(
    offsets_hbm,
    masses_hbm,
    target_hbm,
    leaves_hbm,
    fold_hbm,
    landed,
    leaf_moments,
    tree,
    offsets,
    masses,
    target,
    leaves,
    fold_ref,
    bulk_size,
    slip_size,
    load_sems,
    packed,
    slips,
    got_slips,
    turned,
    raised,
    tiles,
    z_size,
    ready,
    slip_out,
    slip_in,
    bulk_out,
    bulk_in,
    z_out,
    z_in,
    gather_out,
    gather_in,
    core_out,
    core_in,
):
    me = lax.axis_index("curve")
    x = lax.axis_index("rep")
    y, z, c = me // 32, (me // 2) % NZ, me % 2
    rank8 = c * NX + x

    def place(py, pz, pc):
        return (py * NZ + pz) * 2 + pc

    barrier = pltpu.get_barrier_semaphore()
    near = [(dy, dc) for dy in range(NY) for dc in range(2) if dy or dc]
    for dz in (8, 7, 9, 6, 10, 5, 11, 4, 12, 3, 13, 2, 14, 1, 15):
        pl.semaphore_signal(
            barrier,
            inc=1,
            device_id={"curve": place(y, (z + dz) % NZ, c)},
            device_id_type=MESH,
        )
    for dy, dc in near:
        pl.semaphore_signal(
            barrier,
            inc=1,
            device_id={"curve": place((y + dy) % NY, z, (c + dc) % 2)},
            device_id_type=MESH,
        )
    group = [(dx, dc) for dx in range(NX) for dc in range(2) if dx or dc]
    for dx, dc in group:
        if dx:
            pl.semaphore_signal(
                barrier,
                inc=1,
                device_id={"curve": place(y, z, (c + dc) % 2), "rep": (x + dx) % NX},
                device_id_type=MESH,
            )

    loads = [
        pltpu.make_async_copy(source, kept, load_sems.at[index])
        for index, (source, kept) in enumerate(
            (
                (target_hbm, target),
                (leaves_hbm, leaves),
                (masses_hbm, masses),
                (offsets_hbm, offsets),
                (fold_hbm, fold_ref),
            )
        )
    ]
    for load in loads:
        load.start()

    for load in loads:
        load.wait()

    aim = target[...]
    leaf = leaves[...]
    named = ones_where(iota((PEERS, 128), 0) == aim)
    earlier = ones_where(iota((128, 128), 0) < iota((128, 128), 1))
    before = dot(named, earlier, NN)
    within = jnp.sum(before * named.astype(jnp.float32), axis=0, keepdims=True)
    slot = 2 * aim + within.astype(jnp.int32)

    planes = [offsets[0], offsets[1], offsets[2], masses[...]]
    moments = particle_moments(planes, fold_ref[...].astype(jnp.bfloat16))
    moments = jnp.where(iota((64, 128), 0) == TERMS, leaf.astype(jnp.float32), moments)
    nothing = jnp.zeros_like(moments)
    halves = jnp.concatenate(
        [
            jnp.concatenate([moments, nothing], axis=1),
            jnp.concatenate([nothing, moments], axis=1),
        ],
        axis=0,
    )
    twice = 2 * iota((128, 128), 0)
    picks = jnp.concatenate([ones_where(slot == twice), ones_where(slot == twice + 1)], axis=1)
    slips[...] = dot_right(picks, halves, NT)

    pl.semaphore_wait(barrier, 28)
    for dy, dc in near:
        pl.semaphore_signal(
            ready,
            inc=1,
            device_id={"curve": place((y + dy) % NY, z, (c + dc) % 2)},
            device_id_type=MESH,
        )

    spread = ones_where(iota((256, 128), 0) == slot)
    for index, plane in enumerate(planes):
        packed[index] = dot_right(spread, plane)

    def peer(step, inner):
        dz = NZ // 2 + (1 - step % 2) * (step // 2) - (step % 2) * ((step + 1) // 2)
        return place((y + inner // 2) % NY, (z + dz) % NZ, (c + inner % 2) % 2)

    def send_slip(to):
        pltpu.make_async_remote_copy(
            slips.at[pl.ds(to, 1)],
            got_slips.at[pl.ds(me, 1)],
            slip_out,
            slip_in,
            device_id={"curve": to},
            device_id_type=MESH,
        ).start()

    def send_block(to):
        pltpu.make_async_remote_copy(
            packed.at[:, pl.ds(2 * to, 2)],
            landed.at[:, pl.ds(2 * me, 2)],
            bulk_out,
            bulk_in,
            device_id={"curve": to},
            device_id_type=MESH,
        ).start()

    def along_z(send):
        def body(step, carry):
            send(peer(step, 0))
            return carry

        lax.fori_loop(0, NZ - 1, body, 0)

    def all_others(send):
        def body(step, carry):
            send(peer(step // 7, 7 - step % 7))
            return carry

        lax.fori_loop(0, 7 * NZ, body, 0)

    along_z(send_slip)
    pl.semaphore_wait(ready, 7)
    all_others(send_slip)
    along_z(send_block)
    pltpu.make_async_copy(
        slips.at[pl.ds(me, 1)], got_slips.at[pl.ds(me, 1)], slip_in
    ).start()

    pltpu.make_async_copy(
        packed.at[:, pl.ds(2 * me, 2)], landed.at[:, pl.ds(2 * me, 2)], bulk_in
    ).start()

    pltpu.make_async_copy(got_slips, got_slips, slip_in).wait()
    turned[...] = jnp.transpose(got_slips[...])
    cell = jnp.concatenate(
        [turned[TERMS : TERMS + 1], turned[64 + TERMS : 65 + TERMS]], axis=1
    ).astype(jnp.int32)
    rows = [
        jnp.concatenate([turned[r : r + 1], turned[64 + r : 65 + r]], axis=1)
        for r in range(TERMS)
    ]
    raised[...] = jnp.zeros_like(raised)
    for r, row in enumerate(lifted(rows, signs(cell, 2), 2)):
        raised[r : r + 1] = row
    for r, row in enumerate(lifted(rows, signs(cell, 3), 3)):
        for first in (64 + SPARE, 64 + SPARE + TERMS):
            raised[first + r : first + r + 1] = row
    level_two = dot_left(
        raised[0:ROWS], ones_where(iota((128, 256), 0) % 16 == cell >> 6), NT
    )
    upper = dot_right(ones_where(iota((8, 256), 0) == cell >> 9), raised[64:192], NT)
    own_lanes = iota((8, 128), 1) // 16 == iota((8, 128), 0)
    flat = [
        jnp.sum(
            jnp.where(own_lanes, level_two[8 * row : 8 * row + 8], 0.0),
            axis=0,
            keepdims=True,
        )
        for row in range(TILE_ROWS)
    ]
    lane = iota((1, 128), 1)
    flat[4] = jnp.where(
        lane < SPARE, flat[4], jnp.where(lane < SPARE + TERMS, upper[0:1], upper[1:2])
    )
    for row in range(TILE_ROWS):
        tiles[y, z // 8, z % 8, row, pl.ds(rank8, 1)] = flat[row]

    def to_z(dz, carry):
        mine = tiles.at[y, z // 8, z % 8, :, pl.ds(rank8, 1)]
        pltpu.make_async_remote_copy(
            mine,
            mine,
            z_out,
            z_in,
            device_id={"curve": place(y, (z + dz) % NZ, c)},
            device_id_type=MESH,
        ).start()
        return carry

    lax.fori_loop(1, NZ, to_z, 0)
    def mixed(step, carry):
        send_block(peer((step // 7) * 3 % NZ, 7 - step % 7))
        return carry

    lax.fori_loop(0, 7 * NZ, mixed, 0)

    held = jnp.concatenate([turned[:ROWS], turned[64 : 64 + ROWS]], axis=1)
    leaf_moments[...] = dot_left(
        held, ones_where(iota((LEAVES_DEV, 256), 0) == cell), NT
    )[:TERMS]

    pltpu.make_async_copy(z_size, z_size, z_in).wait()

    def spread_tiles(along_y, along_x, turn):
        for step in range(1, NY):
            pltpu.make_async_remote_copy(
                along_y,
                along_y,
                gather_out.at[turn],
                gather_in.at[turn],
                device_id={"curve": place((y + step) % NY, z, c)},
                device_id_type=MESH,
            ).start()
            pltpu.make_async_remote_copy(
                along_x,
                along_x,
                gather_out.at[turn + 1],
                gather_in.at[turn + 1],
                device_id={"rep": (x + step) % NX},
                device_id_type=MESH,
            ).start()

    spread_tiles(
        tiles.at[y, 0, :, :, pl.ds(rank8, 1)],
        tiles.at[y, 1, :, :, pl.ds(rank8, 1)],
        0,
    )
    small = tiles.at[pl.ds(0, 3), 0, :, :, pl.ds(0, 1)]
    pltpu.make_async_copy(small, small, gather_in.at[0]).wait()
    pltpu.make_async_copy(small, small, gather_in.at[1]).wait()
    spread_tiles(
        tiles.at[y, 1, :, :, pl.ds(c * NX, NX)],
        tiles.at[:, 0, :, :, pl.ds(rank8, 1)],
        2,
    )
    large_y = tiles.at[pl.ds(0, 3), 1, :, :, pl.ds(0, 4)]
    large_x = tiles.at[pl.ds(0, 3), 0, :, :, pl.ds(0, 4)]
    pltpu.make_async_copy(large_x, large_x, gather_in.at[3]).wait()
    swaps = []
    for half in range(2):
        if half:
            pltpu.make_async_copy(large_y, large_y, gather_in.at[2]).wait()
        mine = tiles.at[:, half, :, :, pl.ds(c * NX, NX)]
        swap = pltpu.make_async_remote_copy(
            mine,
            mine,
            core_out.at[half],
            core_in.at[half],
            device_id={"curve": place(y, z, 1 - c)},
            device_id_type=MESH,
        )
        swap.start()
        swaps.append(swap)

    for half in range(2):
        swaps[half].wait_recv()

        def write_column(index, carry, half=half):
            at_y, at_z = index // 8, index % 8
            column = at_y * NZ + half * 8 + at_z
            at = pl.ds(pl.multiple_of(column * 128, 128), 128)
            for row in range(5):
                whole = turn_blocks(tiles[at_y, half, at_z, row])
                if row < 4:
                    tree[8 * row : 8 * row + 8, at] = whole
                else:
                    tree[32:35, at] = whole[:3]
            return carry

        lax.fori_loop(0, NY * 8, write_column, 0)
    pairs = jnp.transpose(tiles[:, :, :, 4].reshape(512, 128))
    stacked = jnp.concatenate(
        [
            jnp.concatenate(
                [
                    pairs[SPARE : SPARE + ROWS, 64 * j : 64 * j + 64],
                    pairs[SPARE + TERMS : SPARE + TERMS + ROWS, 64 * j : 64 * j + 64],
                ],
                axis=1,
            )
            for j in range(8)
        ],
        axis=0,
    )
    wide = iota((128, 128), 0)
    thin = iota((128, 128), 1)
    folded = dot_left(stacked, ones_where(2 * (wide % 64) + wide // 64 == thin))
    whole_three = jnp.concatenate([folded[j * ROWS : (j + 1) * ROWS] for j in range(8)], axis=1)
    tree[:, 8192:9216] = whole_three[:TERMS]
    below = [tree[r : r + 1, 8192:9216] for r in range(TERMS)]
    four = jnp.concatenate(lifted(below, signs(iota((1, 1024), 1), 1), 1), axis=0)
    eight = iota((1024, 128), 0) // 8 == iota((1024, 128), 1)
    tree[:, 9216:9344] = dot_left(four, ones_where(eight))

    pltpu.make_async_copy(landed, landed, bulk_in).wait()
    pltpu.make_async_copy(bulk_size, bulk_size, bulk_out).wait()
    pltpu.make_async_copy(slip_size, slip_size, slip_out).wait()
    pltpu.make_async_copy(z_size, z_size, z_out).wait()
    pltpu.make_async_copy(small, small, gather_out.at[0]).wait()
    pltpu.make_async_copy(small, small, gather_out.at[1]).wait()
    pltpu.make_async_copy(large_y, large_y, gather_out.at[2]).wait()
    pltpu.make_async_copy(large_x, large_x, gather_out.at[3]).wait()
    for swap in swaps:
        swap.wait_send()


def store(landed, leaf_moments, tree, places, weights, leaf_out, tree_out, sems):
    steps = [(landed.at[p], places.at[p]) for p in range(3)]
    steps.append((landed.at[3], weights))
    for part in range(5):
        rows = pl.ds(8 * part, 8 if part < 4 else 3)
        steps.append((tree.at[rows], tree_out.at[rows]))
    steps.append((leaf_moments, leaf_out))
    copies = [
        pltpu.make_async_copy(kept, target, sems.at[index])
        for index, (kept, target) in enumerate(steps)
    ]
    for copy in copies:
        copy.start()
    for copy in copies:
        copy.wait()


def shards(offsets, masses, destination, leaf_ids):
    vmem = pl.BlockSpec(memory_space=pltpu.VMEM)
    operands = (
        jnp.transpose(offsets, (1, 0, 2)),
        masses,
        destination.reshape(1, 128),
        leaf_ids.reshape(1, 128),
        jnp.asarray(fold_table()),
    )
    landed, leaf_moments, tree = pl.pallas_call(
        exchange,
        out_shape=(
            jax.ShapeDtypeStruct((4, 256, 256), jnp.float32),
            jax.ShapeDtypeStruct((TERMS, LEAVES_DEV), jnp.float32),
            jax.ShapeDtypeStruct((TERMS, 9344), jnp.float32),
        ),
        in_specs=[pl.BlockSpec(memory_space=pltpu.HBM)] * 5,
        out_specs=(vmem,) * 3,
        scratch_shapes=[
            pltpu.VMEM((3, 128, 256), jnp.float32),
            pltpu.VMEM((128, 256), jnp.float32),
            pltpu.VMEM((1, 128), jnp.int32),
            pltpu.VMEM((1, 128), jnp.int32),
            pltpu.VMEM((64, TERMS * 8), jnp.float32),
            pltpu.VMEM((PEERS - 1, 8, 256), jnp.float32),
            pltpu.VMEM((PEERS - 1, 1, 128), jnp.float32),
            pltpu.SemaphoreType.DMA((5,)),
            pltpu.VMEM((4, 256, 256), jnp.float32),
            pltpu.VMEM((PEERS, 128), jnp.float32),
            pltpu.VMEM((PEERS, 128), jnp.float32),
            pltpu.VMEM((PEERS, 128), jnp.float32),
            pltpu.VMEM((192, 256), jnp.float32),
            pltpu.VMEM((NY, 2, 8, TILE_ROWS, 8, 128), jnp.float32),
            pltpu.VMEM(((NZ - 1) * TILE_ROWS, 1, 128), jnp.float32),
            pltpu.SemaphoreType.REGULAR,
        ]
        + [pltpu.SemaphoreType.DMA] * 6
        + [pltpu.SemaphoreType.DMA((4,))] * 2
        + [pltpu.SemaphoreType.DMA((2,))] * 2,
        compiler_params=pltpu.CompilerParams(
            collective_id=1, has_side_effects=True, vmem_limit_bytes=40 * 1024 * 1024
        ),
        name="exchange",
    )(*[pltpu.with_memory_space_constraint(operand, pltpu.HBM) for operand in operands])
    places, weights, leaf_moments, tree = pl.pallas_call(
        store,
        out_shape=(
            jax.ShapeDtypeStruct((3, 256, 256), jnp.float32),
            jax.ShapeDtypeStruct((256, 256), jnp.float32),
            jax.ShapeDtypeStruct((TERMS, LEAVES_DEV), jnp.float32),
            jax.ShapeDtypeStruct((TERMS, 9344), jnp.float32),
        ),
        in_specs=[vmem] * 3,
        out_specs=(pl.BlockSpec(memory_space=pl.ANY),) * 4,
        scratch_shapes=[pltpu.SemaphoreType.DMA((10,))],
        compiler_params=pltpu.CompilerParams(vmem_limit_bytes=40 * 1024 * 1024),
        name="store",
    )(landed, leaf_moments, tree)
    return jnp.transpose(places, (1, 0, 2)), weights, leaf_moments, tree


def solution(mesh):
    placed = (
        P(("curve", "rep"), None, None),
        P(("curve", "rep"), None),
        P(("curve", "rep"), None),
        P(("curve", "rep")),
    )
    return jax.shard_map(
        shards,
        mesh=mesh,
        in_specs=placed,
        out_specs=(
            P(("curve", "rep"), None, None),
            P(("curve", "rep"), None),
            P(None, ("curve", "rep")),
            P(),
        ),
        check_vma=False,
    )
```
